32 devices in a mesh: group: 2 (over x), expert: 16 (over z, y, core).
Axes of the slice: x: 2, y: 2, z: 4, core: 2. Of those that a mesh axis runs over, the one named last changes fastest.
Arguments:
- tokens: bfloat16 [2048, 1792], P(('group', 'expert')), parts along dimension 0, may hold values from -6 to 6
- shared_gate: bfloat16 [1792, 20480], P(None, 'expert'), may hold values from -0.125 to 0.125
- shared_up: bfloat16 [1792, 20480], P(None, 'expert'), may hold values from -0.125 to 0.125
- shared_down: bfloat16 [20480, 1792], P('expert'), may hold values from -0.0390625 to 0.0390625
- slab_gate: bfloat16 [16, 1792, 640], P('expert'), may hold values from -0.125 to 0.125
- slab_up: bfloat16 [16, 1792, 640], P('expert'), may hold values from -0.125 to 0.125
- slab_down: bfloat16 [16, 640, 1792], P('expert'), may hold values from -0.15625 to 0.15625
- picks: int32 [16, 16, 16], P('group', 'expert'), parts along dimension 0, may hold values from 0 to 63, as said below
- counts: int32 [16, 16], P('group', 'expert'), parts along dimension 0, may hold values from 1 to 16, 128 in all within a row
- gates: float32 [16, 16, 16], P('group', 'expert'), parts along dimension 0, may hold values from 0.1 to 1
Outputs:
- layer_out: bfloat16 [2048, 1792], P(('group', 'expert')), parts along dimension 0
The draws below stay inside these ranges and needn't reach their ends.
There are 2 independent parts, one for each index of `group`. The reference program is written for one: setup_inputs(seed, part) draws one part's arguments, and reference() takes and returns one part's arrays. A program takes and returns all parts, laid end to end along the dimension named above; an argument that names none is the same for every part. Nothing has to cross between parts.
Inputs may be any that keep to these rules, and one draw needn't show every extreme that they name: `picks`: for each expert and source device the 16 entries are distinct rows; entries at or beyond that pair's count are ignored. For each expert the counts over the 16 source devices sum to 128.
All inputs are finite; a program needn't handle non-finite values.
Results may differ from the reference program's by a relative error of at most 0.0053.
Values may be sent and summed in bfloat16 or wider, within the bound.
A program may use at most 192 MiB of HBM per device.

```python
import math
import jax
import jax.numpy as jnp
import numpy as np
from jax import lax

D = 1792
HE = 1280
SH = 20480
TOK_DEV = 64
TOKENS = 1024
SLABS = 16
EXPERTS = 8
HS = 640
CAP = 128
CPAIR = 16


def draw_picks(key, part):
    key = jax.random.fold_in(key, 7)
    pair_keys = jax.random.split(key, EXPERTS * SLABS)
    chosen = jax.vmap(lambda single: jax.random.permutation(single, TOK_DEV)[:CPAIR])(pair_keys)
    return chosen.reshape(EXPERTS, SLABS, CPAIR).astype(jnp.int32)


def block_scale(stream_key, shape, cuts, least, top_value):
    def one(position, parts):
        draws = jax.random.uniform(jax.random.fold_in(jax.random.fold_in(stream_key, 6), position), (parts,), jnp.float32, least / len(cuts), top_value / len(cuts))
        return jnp.repeat(jnp.exp(draws), shape[position] // parts).reshape((-1,) + (1,) * (len(shape) - position - 1))

    level = one(*cuts[0])
    for cut in cuts[1:]:
        level = level * one(*cut)
    return level


def length_profile(count, total, bound, slope):
    loads = [(1 << 20) // math.isqrt(grade ** slope) + 1 for grade in range(2, count + 1)]
    surplus, given = total - bound - (count - 1), [1] * (count - 1)
    while surplus > 0:
        candidates = [i for i in range(count - 1) if given[i] < bound]
        mass, left = sum([loads[i] for i in candidates]), surplus
        for i in candidates:
            addition = min(bound - given[i], max(1, left * loads[i] // mass), surplus)
            given[i] = given[i] + addition
            surplus = surplus - addition
    return np.array([bound] + given)


def ragged(key, amount, total, limit, skew):
    if amount == 2:
        one = jax.random.randint(key, (), max(1, total - limit), min(limit, total - 1) + 1)
        return jnp.stack([one, total - one])
    tallies = jnp.asarray(length_profile(amount, total, limit, skew), jnp.int32)
    couples = (amount - 1) // 2
    source_of, receiver = tallies[1:1 + 2 * couples:2], tallies[2:2 + 2 * couples:2]
    slack = jnp.minimum(source_of - 1, limit - receiver)
    moved = jax.random.randint(jax.random.fold_in(key, 1), (couples,), 0, 1 << 20) % (slack + 1)
    tallies = tallies.at[1:1 + 2 * couples:2].set(source_of - moved).at[2:2 + 2 * couples:2].set(receiver + moved)
    return tallies[jax.random.permutation(jax.random.fold_in(key, 2), amount)]


def normal_values(key, shape, scale, limit, cuts=(), kind=jnp.bfloat16):
    factor_of = block_scale(key, shape, cuts, -0.22, 0.18) if cuts else 1.0
    array = jax.random.normal(key, shape, jnp.float32) * scale * factor_of
    return jnp.minimum(jnp.maximum(array, -limit), limit).astype(kind)


def setup_inputs(seed: int = 0, part: int = 0) -> dict:
    arg_keys = jax.random.split(jax.random.key(seed), 11)
    own_keys = jax.random.split(jax.random.fold_in(arg_keys[10], part), 11)
    tokens = normal_values(own_keys[0], (TOKENS, D), 1.0, 6.0, ((0, 16),))
    shared_gate = normal_values(arg_keys[1], (D, SH), D ** -0.5, 0.125, ((1, 16),))
    shared_up = normal_values(arg_keys[2], (D, SH), D ** -0.5, 0.125, ((1, 16),))
    shared_down = normal_values(arg_keys[3], (SH, D), SH ** -0.5, 0.0390625, ((0, 16),))
    slab_gate = normal_values(arg_keys[4], (SLABS, D, HS), D ** -0.5, 0.125, ((0, 16),))
    slab_up = normal_values(arg_keys[5], (SLABS, D, HS), D ** -0.5, 0.125, ((0, 16),))
    slab_down = normal_values(arg_keys[6], (SLABS, HS, D), HE ** -0.5, 0.15625, ((0, 16),))
    picks = draw_picks(jax.random.fold_in(jax.random.fold_in(arg_keys[10], part), 71), part)
    counts = jax.vmap(lambda own: ragged(own, SLABS, CAP, CPAIR, 2))(jax.random.split(own_keys[8], EXPERTS)).reshape((EXPERTS, SLABS)).astype(jnp.int32)
    gates = jnp.clip(jnp.exp(math.log(1.0) - 2.3025851 * jax.random.uniform(own_keys[9], (EXPERTS, SLABS, CPAIR), jnp.float32) ** block_scale(own_keys[9], (EXPERTS, SLABS, CPAIR), ((1, 16),), -0.2, 0.2)), 0.1, 1.0)
    return dict(tokens=tokens, shared_gate=shared_gate, shared_up=shared_up, shared_down=shared_down, slab_gate=slab_gate, slab_up=slab_up, slab_down=slab_down, picks=picks, counts=counts, gates=gates)


def reference(tokens, shared_gate, shared_up, shared_down, slab_gate, slab_up, slab_down, picks, counts, gates):
    slot_index = lax.broadcasted_iota(jnp.int32, picks.shape, 2)
    live_slot = slot_index < counts[:, :, None]
    owner = (jnp.arange(SLABS, dtype=jnp.int32) * TOK_DEV)[None, :, None] + picks
    kept = jnp.where(live_slot, gates, jnp.zeros((), gates.dtype))
    gate_total = jax.ops.segment_sum(kept.reshape(-1), owner.reshape(-1), num_segments=TOKENS)
    divisor = jnp.maximum(gate_total, 1.0)
    weight = jnp.where(live_slot, gates / divisor[owner], jnp.zeros((), gates.dtype)).astype(jnp.bfloat16)
    gate_act = jnp.dot(tokens, shared_gate, preferred_element_type=jnp.float32)
    up_act = jnp.dot(tokens, shared_up, preferred_element_type=jnp.float32)
    shared_hidden = (jax.nn.silu(gate_act) * up_act).astype(jnp.bfloat16)
    shared_part = jnp.dot(shared_hidden, shared_down, preferred_element_type=jnp.float32)

    def one_slab(routed, pieces):
        w_gate, w_up, w_down, slab_owner, slab_live, slab_weight = pieces
        picked = jnp.where(slab_live[:, :, None], tokens[slab_owner], jnp.zeros((), tokens.dtype))
        flat_rows = picked.reshape(-1, tokens.shape[1])
        hidden = (jax.nn.silu(jnp.dot(flat_rows, w_gate, preferred_element_type=jnp.float32))
                  * jnp.dot(flat_rows, w_up, preferred_element_type=jnp.float32)).astype(jnp.bfloat16)
        output = jnp.dot(hidden, w_down, preferred_element_type=jnp.float32)
        contribution = (output * slab_weight.reshape(-1, 1).astype(jnp.float32)).astype(jnp.bfloat16)
        routed = routed.at[slab_owner.reshape(-1)].add(contribution.astype(jnp.float32))
        return routed, None

    pieces = (slab_gate, slab_up, slab_down, jnp.repeat(owner, 2, axis=0),
              jnp.repeat(live_slot, 2, axis=0), jnp.repeat(weight, 2, axis=0))
    routed, _ = lax.scan(one_slab, jnp.zeros((TOKENS, tokens.shape[1]), jnp.float32), pieces)
    return (shared_part + routed).astype(jnp.bfloat16)
```

```python
import jax
import jax.numpy as jnp
from jax import lax
from jax.experimental import pallas as pl
from jax.experimental.pallas import tpu as pltpu
from jax.sharding import PartitionSpec as P

LINE = 4
LANES = 128
F32 = jnp.float32
BF16 = jnp.bfloat16


def dot(a, b):
    return jnp.dot(a, b, preferred_element_type=F32)


def silu_mul(g, u):
    return g / (1.0 + jnp.exp(-g)) * u


def routing_columns(picks_ref, counts_ref, gates_ref, rows):
    experts, _, slots = picks_ref.shape
    row = lax.broadcasted_iota(jnp.int32, (rows, slots), 0)
    slot = lax.broadcasted_iota(jnp.int32, (rows, slots), 1)
    lane = lax.broadcasted_iota(jnp.int32, (rows, LANES), 1)
    total = jnp.zeros((rows, 1), F32)
    columns = []
    for e in range(experts):
        hit = (picks_ref[e] == row) & (slot < counts_ref[e : e + 1, :])
        gate = jnp.sum(jnp.where(hit, gates_ref[e], 0.0), axis=1, keepdims=True)
        code = jnp.sum(jnp.where(hit, (slot + 1).astype(F32), 0.0), axis=1, keepdims=True)
        total = total + gate
        columns.append((gate, code))
    divisor = jnp.maximum(total, 1.0)
    meta = jnp.zeros((rows, LANES), F32)
    for e, (gate, code) in enumerate(columns):
        meta = jnp.where(lane == e, gate / divisor, meta)
        meta = jnp.where(lane == experts + e, code, meta)
    return meta.astype(BF16)


def kernel(
    tokens, shared_gate, shared_up, shared_down, slab_gate, slab_up, slab_down, picks, counts, gates,
    out,
    w_gate, w_up, w_down, r_gate, r_up, r_down,
    tok, hidden, routed_x, routed_hidden, routed_out, scatter,
    part, core_in, y_out, y_in, y_keep, z_out, z_in,
    load_sem, tok_recv, up_send, down_send, y_send, c_send, c_send_y,
    rc_send, rc_recv, ry_send, ry_recv, rz_send, rz_recv,
):
    me = lax.axis_index("expert")
    z, y, c = me // 4, (me // 2) % 2, me % 2
    half = z // 2
    near = z + half * (3 - 2 * z)
    experts, _, slots = picks.shape
    rows, width = tokens.shape
    expert = me // 2
    y_peer, c_peer = me + 2 - 4 * y, me + 1 - 2 * c

    def mirror(o):
        return o + half * (3 - 2 * o)

    arrive = [mirror(near), mirror(1 - near), mirror(2), mirror(3)]
    leave = [mirror(3), mirror(2 - 2 * near), mirror(1 + near), mirror(near)]

    own = pltpu.make_async_copy(tokens, tok.at[me, :, :width], load_sem.at[6])
    own.start()
    loads = [
        pltpu.make_async_copy(src, dst, load_sem.at[i])
        for i, (src, dst) in enumerate(
            [
                (shared_gate, w_gate),
                (shared_up, w_up),
                (slab_gate.at[0], r_gate),
                (slab_up.at[0], r_up),
                (slab_down.at[0], r_down),
                (shared_down, w_down),
            ]
        )
    ]
    barrier = pltpu.get_barrier_semaphore()

    def greet(target):
        pl.semaphore_signal(barrier, inc=1, device_id={"expert": target})

    greet(y_peer)
    greet(c_peer)

    @pl.when(z < LINE - 1)
    def _():
        greet(me + 4)

    @pl.when(z > 0)
    def _():
        greet(me - 4)

    for load in loads:
        load.start()
    meta = routing_columns(picks, counts, gates, rows)
    own.wait()
    tok[me, :, width:] = meta
    pl.semaphore_wait(barrier, 3 + near)

    def block_copy(s, target, send_sem):
        return pltpu.make_async_remote_copy(
            src_ref=tok.at[s], dst_ref=tok.at[s], send_sem=send_sem, recv_sem=tok_recv.at[s],
            device_id={"expert": target},
        )

    def column_copies(zt, act, along=True):
        s = zt * 4 + y * 2 + c

        if along:

            @pl.when((zt <= z) & (z < LINE - 1))
            def _():
                act(block_copy(s, me + 4, up_send.at[zt]))

            @pl.when((zt >= z) & (z > 0))
            def _():
                act(block_copy(s, me - 4, down_send.at[zt]))

        act(block_copy(s, y_peer, y_send.at[zt]))
        act(block_copy(s, c_peer, c_send.at[zt]))

    def start(copy):
        copy.start()

    def wait_send(copy):
        copy.wait_send()

    def got(s):
        block_copy(s, c_peer, c_send.at[0]).wait_recv()

    def line_step(zt):
        got(zt * 4 + y * 2 + c)
        column_copies(zt, start)

    def layer_ready(zt):
        s = zt * 4 + (1 - y) * 2 + c
        got(s)
        block_copy(s, c_peer, c_send_y.at[zt]).start()
        got(zt * 4 + 1 - c)
        got(zt * 4 + 3 - c)

    def first_half(zt):
        def tile(n, _):
            columns = pl.ds(pl.multiple_of(n * 256, 256), 256)
            x = tok[pl.ds(zt * 4, 4), :, :width].reshape(4 * rows, width)
            g = dot(x, w_gate[:, columns])
            u = dot(x, w_up[:, columns])
            hidden[zt, :, columns] = silu_mul(g, u).astype(BF16)
            return 0

        lax.fori_loop(0, w_gate.shape[1] // 256, tile, 0)
        info = tok[pl.ds(zt * 4, 4), :, width:].reshape(4 * rows, LANES)
        slots4 = 4 * slots
        lane_r = lax.broadcasted_iota(jnp.int32, (slots4, LANES), 1)
        pick_code = jnp.where(lane_r == experts + expert, 1.0, 0.0).astype(BF16)
        pick_weight = jnp.where(lane_r == expert, 1.0, 0.0).astype(BF16)
        nt = (((1,), (1,)), ((), ()))
        code_t = lax.dot_general(pick_code, info, nt, preferred_element_type=F32)
        code = lax.dot_general(info, pick_code, nt, preferred_element_type=F32)
        weight = lax.dot_general(info, pick_weight, nt, preferred_element_type=F32)

        def match(codes, slot_dim):
            slot = lax.broadcasted_iota(jnp.int32, codes.shape, slot_dim)
            token = lax.broadcasted_iota(jnp.int32, codes.shape, 1 - slot_dim)
            return (codes == (slot % slots + 1).astype(F32)) & (slot // slots == token // rows)

        scatter[zt] = jnp.where(match(code, 1), weight, 0.0).astype(BF16)
        gather = jnp.where(match(code_t, 0), 1.0, 0.0).astype(BF16)
        x = tok[pl.ds(zt * 4, 4), :, :width].reshape(4 * rows, width)
        routed_x[zt] = dot(gather, x).astype(BF16)

    column_copies(arrive[0], start)
    line_step(arrive[1])

    @pl.when(near == 1)
    def _():
        line_step(arrive[2])

    layer_ready(arrive[0])
    loads[0].wait()
    loads[1].wait()
    first_half(arrive[0])

    @pl.when(near == 0)
    def _():
        line_step(arrive[2])

    layer_ready(arrive[1])
    first_half(arrive[1])
    line_step(arrive[3])
    layer_ready(arrive[2])
    first_half(arrive[2])
    layer_ready(arrive[3])
    first_half(arrive[3])

    for load in loads[2:]:
        load.wait()
    picked = LINE * 4 * slots
    hs = r_gate.shape[1]
    for low in range(0, hs, 256):
        high = min(hs, low + 256)
        x = routed_x[...].reshape(picked, width)
        g = dot(x, r_gate[:, low:high])
        u = dot(x, r_up[:, low:high])
        routed_hidden[:, low:high] = silu_mul(g, u).astype(BF16)

    def routed_tile(n, _):
        columns = pl.ds(pl.multiple_of(n * 256, 256), 256)
        o = dot(routed_hidden[...], r_down[:, columns])
        routed_out[:, :, columns] = o.reshape(LINE, 4 * slots, 256).astype(BF16)
        return 0

    lax.fori_loop(0, width // 256, routed_tile, 0)

    def second_half(zt):
        def tile(n, _):
            columns = pl.ds(pl.multiple_of(n * 256, 256), 256)
            p = dot(hidden[zt], w_down[:, columns]) + dot(scatter[zt], routed_out[zt, :, columns])
            p = p.astype(BF16)
            for b in range(4):
                part[zt, b % 2, b // 2, :, columns] = p[b * rows : (b + 1) * rows]
            return 0

        lax.fori_loop(0, width // 256, tile, 0)

    def core_copy(zt):
        return pltpu.make_async_remote_copy(
            src_ref=part.at[zt, 1 - c], dst_ref=core_in.at[zt], send_sem=rc_send.at[zt],
            recv_sem=rc_recv.at[zt], device_id={"expert": c_peer},
        )

    def y_copy(zt):
        return pltpu.make_async_remote_copy(
            src_ref=y_out.at[zt], dst_ref=y_in.at[zt], send_sem=ry_send.at[zt],
            recv_sem=ry_recv.at[zt], device_id={"expert": y_peer},
        )

    def z_copy(zt, way, target):
        return pltpu.make_async_remote_copy(
            src_ref=z_out.at[zt], dst_ref=z_in.at[way, zt], send_sem=rz_send.at[zt],
            recv_sem=rz_recv.at[way, zt], device_id={"expert": target},
        )

    def y_stage(zt):
        core_copy(zt).wait_recv()
        y_out[zt] = (part[zt, c, 1 - y].astype(F32) + core_in[zt, 1 - y].astype(F32)).astype(BF16)
        y_copy(zt).start()
        y_keep[zt] = part[zt, c, y].astype(F32) + core_in[zt, y].astype(F32)

    def z_stage(zt, last):
        y_copy(zt).wait_recv()
        y_keep[zt] += y_in[zt].astype(F32)

        @pl.when((zt >= z) & (z > 0))
        def _():
            z_copy(zt, 0, me - 4).wait_recv()
            y_keep[zt] += z_in[0, zt].astype(F32)

        @pl.when((zt <= z) & (z < LINE - 1))
        def _():
            z_copy(zt, 1, me + 4).wait_recv()
            y_keep[zt] += z_in[1, zt].astype(F32)

        if last:
            out[...] = y_keep[zt].astype(BF16)
        else:
            z_out[zt] = y_keep[zt].astype(BF16)

            @pl.when(zt > z)
            def _():
                z_copy(zt, 0, me + 4).start()

            @pl.when(zt < z)
            def _():
                z_copy(zt, 1, me - 4).start()

    for i in range(LINE):
        second_half(leave[i])
        core_copy(leave[i]).start()
        if i > 0:
            y_stage(leave[i - 1])
    y_stage(leave[-1])
    for i in range(LINE):
        z_stage(leave[i], i == LINE - 1)

    for i in range(LINE):
        column_copies(arrive[i], wait_send)
        block_copy(arrive[i] * 4 + (1 - y) * 2 + c, c_peer, c_send_y.at[arrive[i]]).wait_send()
        core_copy(leave[i]).wait_send()
        y_copy(leave[i]).wait_send()
        if i < LINE - 1:
            z_copy(leave[i], 0, y_peer).wait_send()


def fused(
    tokens, shared_gate, shared_up, shared_down, slab_gate, slab_up, slab_down, picks, counts, gates
):
    rows, width = tokens.shape
    hid = shared_gate.shape[1]
    hs = slab_gate.shape[2]
    slots = picks.shape[2]
    any_spec = pl.BlockSpec(memory_space=pl.ANY)
    vmem_spec = pl.BlockSpec(memory_space=pltpu.VMEM)
    dma = pltpu.SemaphoreType.DMA
    vm = pltpu.VMEM
    flops = 2 * 16 * rows * width * hid * 3
    return pl.pallas_call(
        kernel,
        out_shape=jax.ShapeDtypeStruct((rows, width), BF16),
        in_specs=[any_spec] * 7 + [vmem_spec] * 3,
        out_specs=vmem_spec,
        scratch_shapes=[
            vm((width, hid), BF16), vm((width, hid), BF16), vm((hid, width), BF16),
            vm((width, hs), BF16), vm((width, hs), BF16), vm((hs, width), BF16),
            vm((4 * LINE, rows, width + LANES), BF16),
            vm((LINE, 4 * rows, hid), BF16),
            vm((LINE, 4 * slots, width), BF16),
            vm((LINE * 4 * slots, hs), BF16),
            vm((LINE, 4 * slots, width), BF16),
            vm((LINE, 4 * rows, 4 * slots), BF16),
            vm((LINE, 2, 2, rows, width), BF16),
            vm((LINE, 2, rows, width), BF16),
            vm((LINE, rows, width), BF16),
            vm((LINE, rows, width), BF16),
            vm((LINE, rows, width), F32),
            vm((LINE, rows, width), BF16),
            vm((2, LINE, rows, width), BF16),
            dma((7,)), dma((4 * LINE,)), dma((LINE,)), dma((LINE,)), dma((LINE,)), dma((LINE,)),
            dma((LINE,)),
            dma((LINE,)), dma((LINE,)), dma((LINE,)), dma((LINE,)), dma((LINE,)), dma((2, LINE)),
        ],
        compiler_params=pltpu.CompilerParams(
            collective_id=0, has_side_effects=True, vmem_limit_bytes=60 * 1024 * 1024
        ),
        cost_estimate=pl.CostEstimate(flops=flops, bytes_accessed=21000000, transcendentals=0),
    )(tokens, shared_gate, shared_up, shared_down, slab_gate, slab_up, slab_down, picks, counts, gates)


def return_routed(contribution, sources, slot_count, features, onehot, experts, tok_dev):
    returned = lax.all_to_all(
        contribution.reshape(sources, slot_count, features),
        "expert",
        split_axis=0,
        concat_axis=0,
        tiled=True,
    )
    owner_table = (
        jnp.repeat(onehot, 2, axis=0)
        .reshape(2 * experts * slot_count, tok_dev)
        .astype(jnp.bfloat16)
    )
    return lax.dot_general(
        owner_table,
        returned.reshape(-1, features),
        (((0,), (0,)), ((), ())),
        preferred_element_type=jnp.float32,
    )


def on_device(
    tokens, shared_gate, shared_up, shared_down, slab_gate, slab_up, slab_down, picks, counts, gates
):
    tok_dev, features = tokens.shape
    own_picks = picks[:, 0, :]
    own_gates = gates[:, 0, :]
    experts, slot_count = own_picks.shape
    live_slot = lax.broadcasted_iota(jnp.int32, (experts, slot_count), 1) < counts
    local_rows = lax.broadcasted_iota(jnp.int32, (1, 1, tok_dev), 2)
    onehot = (own_picks[:, :, None] == local_rows) & live_slot[:, :, None]
    gate_total = jnp.sum(jnp.where(onehot, own_gates[:, :, None], 0.0), axis=(0, 1))
    divisor = jnp.maximum(gate_total, 1.0)
    weight = jnp.where(live_slot, own_gates / divisor[own_picks], 0.0).astype(jnp.bfloat16)
    sent_rows = jnp.where(live_slot[:, :, None], tokens[own_picks], jnp.zeros((), tokens.dtype))
    positions = own_picks.astype(jnp.float32).astype(jnp.bfloat16)
    weight_both = jnp.repeat(weight, 2, axis=0)
    position_both = jnp.repeat(positions, 2, axis=0)
    received, got_weight, got_position = (
        lax.all_to_all(
            jnp.repeat(sent_rows, 2, axis=0), "expert", split_axis=0, concat_axis=0, tiled=True
        ),
        lax.all_to_all(weight_both, "expert", split_axis=0, concat_axis=0, tiled=True),
        lax.all_to_all(position_both, "expert", split_axis=0, concat_axis=0, tiled=True),
    )
    sources = received.shape[0]
    flat_rows = received.reshape(sources * slot_count, features)
    gate_act = jnp.dot(flat_rows, slab_gate[0], preferred_element_type=jnp.float32)
    up_act = jnp.dot(flat_rows, slab_up[0], preferred_element_type=jnp.float32)
    slab_hidden = (jax.nn.silu(gate_act) * up_act).astype(jnp.bfloat16)
    slab_output = jnp.dot(slab_hidden, slab_down[0], preferred_element_type=jnp.float32)
    contribution = (slab_output * got_weight.reshape(-1, 1).astype(jnp.float32)).astype(
        jnp.bfloat16
    )
    piece = lax.all_gather(tokens, "expert", axis=0, tiled=True)
    gate_part = jnp.dot(piece, shared_gate, preferred_element_type=jnp.float32)
    up_part = jnp.dot(piece, shared_up, preferred_element_type=jnp.float32)
    shared_hidden = (jax.nn.silu(gate_part) * up_part).astype(jnp.bfloat16)
    layer_sum = lax.psum_scatter(
        jnp.dot(shared_hidden, shared_down, preferred_element_type=jnp.float32),
        "expert",
        scatter_dimension=0,
        tiled=True,
    )
    layer_sum = layer_sum + return_routed(
        contribution, sources, slot_count, features, onehot, experts, tok_dev
    )
    return layer_sum.astype(jnp.bfloat16)


def solution(mesh):
    in_specs = (
        P(("group", "expert"), None),
        P(None, "expert"),
        P(None, "expert"),
        P("expert", None),
        P("expert", None, None),
        P("expert", None, None),
        P("expert", None, None),
        P("group", "expert", None),
        P("group", "expert"),
        P("group", "expert", None),
    )
    out_specs = P(("group", "expert"), None)
    body = fused if mesh.shape["expert"] == 4 * LINE else on_device
    return jax.shard_map(
        body, mesh=mesh, in_specs=in_specs, out_specs=out_specs, check_vma=False
    )
```

```python
import jax
import jax.numpy as jnp
from jax import lax
from jax.experimental import pallas as pl
from jax.experimental.pallas import tpu as pltpu
from jax.sharding import PartitionSpec as P

LINE = 4
LANES = 128
F32 = jnp.float32
BF16 = jnp.bfloat16


def dot(a, b):
    return jnp.dot(a, b, preferred_element_type=F32)


def silu_mul(g, u):
    return g / (1.0 + jnp.exp(-g)) * u


def routing_columns(picks_ref, counts_ref, gates_ref, rows):
    experts, _, slots = picks_ref.shape
    row = lax.broadcasted_iota(jnp.int32, (rows, slots), 0)
    slot = lax.broadcasted_iota(jnp.int32, (rows, slots), 1)
    lane = lax.broadcasted_iota(jnp.int32, (rows, LANES), 1)
    total = jnp.zeros((rows, 1), F32)
    columns = []
    for e in range(experts):
        hit = (picks_ref[e] == row) & (slot < counts_ref[e : e + 1, :])
        gate = jnp.sum(jnp.where(hit, gates_ref[e], 0.0), axis=1, keepdims=True)
        code = jnp.sum(jnp.where(hit, (slot + 1).astype(F32), 0.0), axis=1, keepdims=True)
        total = total + gate
        columns.append((gate, code))
    divisor = jnp.maximum(total, 1.0)
    meta = jnp.zeros((rows, LANES), F32)
    for e, (gate, code) in enumerate(columns):
        meta = jnp.where(lane == e, gate / divisor, meta)
        meta = jnp.where(lane == experts + e, code, meta)
    return meta.astype(BF16)


def kernel(
    tokens, shared_gate, shared_up, shared_down, slab_gate, slab_up, slab_down, picks, counts, gates,
    out,
    w_gate, w_up, w_down, r_gate, r_up, r_down,
    tok, hidden, routed_x, routed_hidden, routed_out, scatter,
    part, core_in, y_out, y_in, y_keep, z_out, z_in,
    load_sem, tok_recv, up_send, down_send, y_send, c_send, c_send_y,
    rc_send, rc_recv, ry_send, ry_recv, rz_send, rz_recv,
):
    me = lax.axis_index("expert")
    z, y, c = me // 4, (me // 2) % 2, me % 2
    half = z // 2
    near = z + half * (3 - 2 * z)
    experts, _, slots = picks.shape
    rows, width = 2 * tokens.shape[1], tokens.shape[2]
    expert = me // 2
    y_peer, c_peer = me + 2 - 4 * y, me + 1 - 2 * c

    def mirror(o):
        return o + half * (3 - 2 * o)

    arrive = [mirror(near), mirror(1 - near), mirror(2), mirror(3)]
    leave = [arrive[2], arrive[3], arrive[1], arrive[0]]

    own = pltpu.make_async_copy(tokens, tok.at[me, :, :, :width], load_sem.at[6])
    own.start()
    loads = [
        pltpu.make_async_copy(src, dst, load_sem.at[i])
        for i, (src, dst) in enumerate(
            [
                (shared_gate, w_gate),
                (shared_up, w_up),
                (slab_gate.at[0], r_gate),
                (slab_up.at[0], r_up),
                (slab_down.at[0], r_down),
                (shared_down, w_down),
            ]
        )
    ]
    barrier = pltpu.get_barrier_semaphore()

    def greet(target):
        pl.semaphore_signal(barrier, inc=1, device_id={"expert": target})

    greet(y_peer)
    greet(c_peer)

    @pl.when(z < LINE - 1)
    def _():
        greet(me + 4)

    @pl.when(z > 0)
    def _():
        greet(me - 4)

    meta = routing_columns(picks, counts, gates, rows)
    own.wait()
    tok[me, :, :, width:] = meta.reshape(2, rows // 2, LANES)
    pl.semaphore_wait(barrier, 3 + near)

    def block_copy(s, h, target, send_sem):
        return pltpu.make_async_remote_copy(
            src_ref=tok.at[s, h], dst_ref=tok.at[s, h], send_sem=send_sem, recv_sem=tok_recv.at[s, h],
            device_id={"expert": target},
        )

    def column_copies(zt, h, act):
        s = zt * 4 + y * 2 + c

        @pl.when((zt <= z) & (z < LINE - 1))
        def _():
            act(block_copy(s, h, me + 4, up_send.at[zt, h]))

        @pl.when((zt >= z) & (z > 0))
        def _():
            act(block_copy(s, h, me - 4, down_send.at[zt, h]))

        act(block_copy(s, h, y_peer, y_send.at[zt, h]))
        act(block_copy(s, h, c_peer, c_send.at[zt, h]))

    def start(copy):
        copy.start()

    def wait_send(copy):
        copy.wait_send()

    def got(s, h):
        block_copy(s, h, c_peer, c_send.at[0, 0]).wait_recv()

    def line_step(zt, h):
        got(zt * 4 + y * 2 + c, h)
        column_copies(zt, h, start)

    def y_step(zt, h):
        s = zt * 4 + (1 - y) * 2 + c
        got(s, h)
        block_copy(s, h, c_peer, c_send_y.at[zt, h]).start()

    def core_step(zt):
        for h in range(2):
            got(zt * 4 + 1 - c, h)
            got(zt * 4 + 3 - c, h)

    def first_half(i):
        zt = arrive[i]

        def tile(n, _):
            columns = pl.ds(pl.multiple_of(n * 256, 256), 256)
            x = tok[pl.ds(zt * 4, 4), :, :, :width].reshape(4 * rows, width)
            g = dot(x, w_gate[:, columns])
            u = dot(x, w_up[:, columns])
            hidden[zt, :, columns] = silu_mul(g, u).astype(BF16)
            return 0

        lax.fori_loop(0, w_gate.shape[1] // 256, tile, 0)
        info = tok[pl.ds(zt * 4, 4), :, :, width:].reshape(4 * rows, LANES)
        slots4 = 4 * slots
        lane_r = lax.broadcasted_iota(jnp.int32, (slots4, LANES), 1)
        pick_code = jnp.where(lane_r == experts + expert, 1.0, 0.0).astype(BF16)
        pick_weight = jnp.where(lane_r == expert, 1.0, 0.0).astype(BF16)
        nt = (((1,), (1,)), ((), ()))
        code_t = lax.dot_general(pick_code, info, nt, preferred_element_type=F32)
        code = lax.dot_general(info, pick_code, nt, preferred_element_type=F32)
        weight = lax.dot_general(info, pick_weight, nt, preferred_element_type=F32)

        def match(codes, slot_dim):
            slot = lax.broadcasted_iota(jnp.int32, codes.shape, slot_dim)
            token = lax.broadcasted_iota(jnp.int32, codes.shape, 1 - slot_dim)
            return (codes == (slot % slots + 1).astype(F32)) & (slot // slots == token // rows)

        scatter[zt] = jnp.where(match(code, 1), weight, 0.0).astype(BF16)
        gather = jnp.where(match(code_t, 0), 1.0, 0.0).astype(BF16)
        x = tok[pl.ds(zt * 4, 4), :, :, :width].reshape(4 * rows, width)
        routed_x[i * 4 * slots : (i + 1) * 4 * slots] = dot(gather, x).astype(BF16)

    picked = 4 * slots
    hs = r_gate.shape[1]

    def routed(first, count):
        size = count * picked
        base = first * picked
        for low in range(0, hs, 256):
            high = min(hs, low + 256)
            g = dot(routed_x[base : base + size], r_gate[:, low:high])
            u = dot(routed_x[base : base + size], r_up[:, low:high])
            routed_hidden[:size, low:high] = silu_mul(g, u).astype(BF16)

        def tile(n, _):
            columns = pl.ds(pl.multiple_of(n * 256, 256), 256)
            o = dot(routed_hidden[:size], r_down[:, columns]).astype(BF16)
            routed_out[base : base + size, columns] = o
            return 0

        lax.fori_loop(0, width // 256, tile, 0)

    middle = width // 512 * 256
    cuts = ((0, middle), (middle, width - middle))

    def cut(h):
        return pl.ds(*cuts[h])

    def core_copy(zt, h):
        return pltpu.make_async_remote_copy(
            src_ref=part.at[zt, 1 - c, :, :, cut(h)], dst_ref=core_in.at[zt, :, :, cut(h)],
            send_sem=rc_send.at[zt, h], recv_sem=rc_recv.at[zt, h], device_id={"expert": c_peer},
        )

    def y_copy(zt, h):
        return pltpu.make_async_remote_copy(
            src_ref=y_out.at[zt, :, cut(h)], dst_ref=y_in.at[zt, :, cut(h)],
            send_sem=ry_send.at[zt, h], recv_sem=ry_recv.at[zt, h], device_id={"expert": y_peer},
        )

    def z_copy(zt, h, way, target):
        return pltpu.make_async_remote_copy(
            src_ref=z_out.at[zt, :, cut(h)], dst_ref=z_in.at[way, zt, :, cut(h)],
            send_sem=rz_send.at[zt, h], recv_sem=rz_recv.at[way, zt, h], device_id={"expert": target},
        )

    def second_half(i, h):
        zt = arrive[i]

        def tile(n, _):
            columns = pl.ds(pl.multiple_of(n * 256, 256), 256)
            p = dot(hidden[zt], w_down[:, columns]) + dot(scatter[zt], routed_out[i * picked : (i + 1) * picked, columns])
            p = p.astype(BF16)
            for b in range(4):
                part[zt, b % 2, b // 2, :, columns] = p[b * rows : (b + 1) * rows]
            return 0

        low, size = cuts[h]
        lax.fori_loop(low // 256, (low + size) // 256, tile, 0)
        core_copy(zt, h).start()

    def y_stage(zt, h):
        core_copy(zt, h).wait_recv()
        away = part[zt, c, 1 - y, :, cut(h)].astype(F32) + core_in[zt, 1 - y, :, cut(h)].astype(F32)
        y_out[zt, :, cut(h)] = away.astype(BF16)
        y_copy(zt, h).start()
        y_keep[zt, :, cut(h)] = (
            part[zt, c, y, :, cut(h)].astype(F32) + core_in[zt, y, :, cut(h)].astype(F32)
        )

    def z_stage(zt, h, last):
        y_copy(zt, h).wait_recv()
        y_keep[zt, :, cut(h)] += y_in[zt, :, cut(h)].astype(F32)

        @pl.when((zt >= z) & (z > 0))
        def _():
            z_copy(zt, h, 0, me - 4).wait_recv()
            y_keep[zt, :, cut(h)] += z_in[0, zt, :, cut(h)].astype(F32)

        @pl.when((zt <= z) & (z < LINE - 1))
        def _():
            z_copy(zt, h, 1, me + 4).wait_recv()
            y_keep[zt, :, cut(h)] += z_in[1, zt, :, cut(h)].astype(F32)

        if last:
            out[:, cut(h)] = y_keep[zt, :, cut(h)].astype(BF16)
        else:
            z_out[zt, :, cut(h)] = y_keep[zt, :, cut(h)].astype(BF16)

            @pl.when(zt > z)
            def _():
                z_copy(zt, h, 0, me + 4).start()

            @pl.when(zt < z)
            def _():
                z_copy(zt, h, 1, me - 4).start()

    for h in range(2):
        column_copies(arrive[0], h, start)
    for load in loads:
        load.start()
    for h in range(2):
        line_step(arrive[1], h)

        @pl.when(near == 1)
        def _():
            line_step(arrive[2], h)

        y_step(arrive[0], h)
    core_step(arrive[0])
    loads[0].wait()
    loads[1].wait()
    first_half(0)

    for h in range(2):
        line_step(mirror(2 + near), h)
    for h in range(2):
        y_step(arrive[1], h)
    core_step(arrive[1])
    first_half(1)
    for load in loads[2:5]:
        load.wait()
    routed(0, 2)

    for h in range(2):

        @pl.when(near == 0)
        def _():
            line_step(arrive[3], h)

        y_step(arrive[2], h)
    core_step(arrive[2])
    first_half(2)
    routed(2, 1)
    loads[5].wait()

    for h in range(2):
        y_step(arrive[3], h)
        second_half(2, h)
    for h in range(2):
        y_stage(arrive[2], h)
    core_step(arrive[3])
    first_half(3)
    routed(3, 1)
    second_half(3, 0)
    second_half(3, 1)
    y_stage(arrive[3], 0)
    second_half(1, 0)
    y_stage(arrive[3], 1)
    second_half(1, 1)
    y_stage(arrive[1], 0)

    @pl.when(near == 0)
    def _():
        for h in range(2):
            z_stage(arrive[2], h, False)

    second_half(0, 0)
    y_stage(arrive[1], 1)
    second_half(0, 1)
    y_stage(arrive[0], 0)
    y_stage(arrive[0], 1)

    @pl.when(near == 1)
    def _():
        for h in range(2):
            z_stage(arrive[2], h, False)

    for i in range(1, LINE):
        for h in range(2):
            z_stage(leave[i], h, i == LINE - 1)

    for i in range(LINE):
        for h in range(2):
            column_copies(arrive[i], h, wait_send)
            s = arrive[i] * 4 + (1 - y) * 2 + c
            block_copy(s, h, c_peer, c_send_y.at[arrive[i], h]).wait_send()
            core_copy(leave[i], h).wait_send()
            y_copy(leave[i], h).wait_send()
            if i < LINE - 1:
                z_copy(leave[i], h, 0, y_peer).wait_send()


def fused(
    tokens, shared_gate, shared_up, shared_down, slab_gate, slab_up, slab_down, picks, counts, gates
):
    rows, width = tokens.shape
    hid = shared_gate.shape[1]
    hs = slab_gate.shape[2]
    slots = picks.shape[2]
    any_spec = pl.BlockSpec(memory_space=pl.ANY)
    vmem_spec = pl.BlockSpec(memory_space=pltpu.VMEM)
    dma = pltpu.SemaphoreType.DMA
    vm = pltpu.VMEM
    flops = 2 * 16 * rows * width * hid * 3
    return pl.pallas_call(
        kernel,
        out_shape=jax.ShapeDtypeStruct((rows, width), BF16),
        in_specs=[any_spec] * 7 + [vmem_spec] * 3,
        out_specs=vmem_spec,
        scratch_shapes=[
            vm((width, hid), BF16), vm((width, hid), BF16), vm((hid, width), BF16),
            vm((width, hs), BF16), vm((width, hs), BF16), vm((hs, width), BF16),
            vm((4 * LINE, 2, rows // 2, width + LANES), BF16),
            vm((LINE, 4 * rows, hid), BF16),
            vm((LINE * 4 * slots, width), BF16),
            vm((LINE * 4 * slots, hs), BF16),
            vm((LINE * 4 * slots, width), BF16),
            vm((LINE, 4 * rows, 4 * slots), BF16),
            vm((LINE, 2, 2, rows, width), BF16),
            vm((LINE, 2, rows, width), BF16),
            vm((LINE, rows, width), BF16),
            vm((LINE, rows, width), BF16),
            vm((LINE, rows, width), F32),
            vm((LINE, rows, width), BF16),
            vm((2, LINE, rows, width), BF16),
            dma((7,)), dma((4 * LINE, 2)), dma((LINE, 2)), dma((LINE, 2)), dma((LINE, 2)),
            dma((LINE, 2)), dma((LINE, 2)),
            dma((LINE, 2)), dma((LINE, 2)), dma((LINE, 2)), dma((LINE, 2)), dma((LINE, 2)),
            dma((2, LINE, 2)),
        ],
        compiler_params=pltpu.CompilerParams(
            collective_id=0, has_side_effects=True, vmem_limit_bytes=60 * 1024 * 1024
        ),
        cost_estimate=pl.CostEstimate(flops=flops, bytes_accessed=21000000, transcendentals=0),
    )(tokens.reshape(2, rows // 2, width), shared_gate, shared_up, shared_down, slab_gate, slab_up, slab_down, picks, counts, gates)


def return_routed(contribution, sources, slot_count, features, onehot, experts, tok_dev):
    returned = lax.all_to_all(
        contribution.reshape(sources, slot_count, features),
        "expert",
        split_axis=0,
        concat_axis=0,
        tiled=True,
    )
    owner_table = (
        jnp.repeat(onehot, 2, axis=0)
        .reshape(2 * experts * slot_count, tok_dev)
        .astype(jnp.bfloat16)
    )
    return lax.dot_general(
        owner_table,
        returned.reshape(-1, features),
        (((0,), (0,)), ((), ())),
        preferred_element_type=jnp.float32,
    )


def on_device(
    tokens, shared_gate, shared_up, shared_down, slab_gate, slab_up, slab_down, picks, counts, gates
):
    tok_dev, features = tokens.shape
    own_picks = picks[:, 0, :]
    own_gates = gates[:, 0, :]
    experts, slot_count = own_picks.shape
    live_slot = lax.broadcasted_iota(jnp.int32, (experts, slot_count), 1) < counts
    local_rows = lax.broadcasted_iota(jnp.int32, (1, 1, tok_dev), 2)
    onehot = (own_picks[:, :, None] == local_rows) & live_slot[:, :, None]
    gate_total = jnp.sum(jnp.where(onehot, own_gates[:, :, None], 0.0), axis=(0, 1))
    divisor = jnp.maximum(gate_total, 1.0)
    weight = jnp.where(live_slot, own_gates / divisor[own_picks], 0.0).astype(jnp.bfloat16)
    sent_rows = jnp.where(live_slot[:, :, None], tokens[own_picks], jnp.zeros((), tokens.dtype))
    positions = own_picks.astype(jnp.float32).astype(jnp.bfloat16)
    weight_both = jnp.repeat(weight, 2, axis=0)
    position_both = jnp.repeat(positions, 2, axis=0)
    received, got_weight, got_position = (
        lax.all_to_all(
            jnp.repeat(sent_rows, 2, axis=0), "expert", split_axis=0, concat_axis=0, tiled=True
        ),
        lax.all_to_all(weight_both, "expert", split_axis=0, concat_axis=0, tiled=True),
        lax.all_to_all(position_both, "expert", split_axis=0, concat_axis=0, tiled=True),
    )
    sources = received.shape[0]
    flat_rows = received.reshape(sources * slot_count, features)
    gate_act = jnp.dot(flat_rows, slab_gate[0], preferred_element_type=jnp.float32)
    up_act = jnp.dot(flat_rows, slab_up[0], preferred_element_type=jnp.float32)
    slab_hidden = (jax.nn.silu(gate_act) * up_act).astype(jnp.bfloat16)
    slab_output = jnp.dot(slab_hidden, slab_down[0], preferred_element_type=jnp.float32)
    contribution = (slab_output * got_weight.reshape(-1, 1).astype(jnp.float32)).astype(
        jnp.bfloat16
    )
    piece = lax.all_gather(tokens, "expert", axis=0, tiled=True)
    gate_part = jnp.dot(piece, shared_gate, preferred_element_type=jnp.float32)
    up_part = jnp.dot(piece, shared_up, preferred_element_type=jnp.float32)
    shared_hidden = (jax.nn.silu(gate_part) * up_part).astype(jnp.bfloat16)
    layer_sum = lax.psum_scatter(
        jnp.dot(shared_hidden, shared_down, preferred_element_type=jnp.float32),
        "expert",
        scatter_dimension=0,
        tiled=True,
    )
    layer_sum = layer_sum + return_routed(
        contribution, sources, slot_count, features, onehot, experts, tok_dev
    )
    return layer_sum.astype(jnp.bfloat16)


def solution(mesh):
    in_specs = (
        P(("group", "expert"), None),
        P(None, "expert"),
        P(None, "expert"),
        P("expert", None),
        P("expert", None, None),
        P("expert", None, None),
        P("expert", None, None),
        P("group", "expert", None),
        P("group", "expert"),
        P("group", "expert", None),
    )
    out_specs = P(("group", "expert"), None)
    body = fused if mesh.shape["expert"] == 4 * LINE else on_device
    return jax.shard_map(
        body, mesh=mesh, in_specs=in_specs, out_specs=out_specs, check_vma=False
    )
```

```python
import jax
import jax.numpy as jnp
from jax import lax
from jax.experimental import pallas as pl
from jax.experimental.pallas import tpu as pltpu
from jax.sharding import PartitionSpec as P

LINE = 4
LANES = 128
F32 = jnp.float32
BF16 = jnp.bfloat16


def dot(a, b):
    return jnp.dot(a, b, preferred_element_type=F32)


def silu_mul(g, u):
    return g / (1.0 + jnp.exp(-g)) * u


def routing_columns(picks_ref, counts_ref, gates_ref, rows):
    experts, _, slots = picks_ref.shape
    row = lax.broadcasted_iota(jnp.int32, (rows, slots), 0)
    slot = lax.broadcasted_iota(jnp.int32, (rows, slots), 1)
    lane = lax.broadcasted_iota(jnp.int32, (rows, LANES), 1)
    total = jnp.zeros((rows, 1), F32)
    columns = []
    for e in range(experts):
        hit = (picks_ref[e] == row) & (slot < counts_ref[e : e + 1, :])
        gate = jnp.sum(jnp.where(hit, gates_ref[e], 0.0), axis=1, keepdims=True)
        code = jnp.sum(jnp.where(hit, (slot + 1).astype(F32), 0.0), axis=1, keepdims=True)
        total = total + gate
        columns.append((gate, code))
    divisor = jnp.maximum(total, 1.0)
    meta = jnp.zeros((rows, LANES), F32)
    for e, (gate, code) in enumerate(columns):
        meta = jnp.where(lane == e, gate / divisor, meta)
        meta = jnp.where(lane == experts + e, code, meta)
    return meta.astype(BF16)


def kernel(
    tokens, shared_gate, shared_up, shared_down, slab_gate, slab_up, slab_down, picks, counts, gates,
    out,
    w_gate, w_up, w_down, r_gate, r_up, r_down,
    tok, hidden, routed_x, routed_hidden, routed_out, scatter,
    part, core_in, y_out, y_in, y_keep, z_out, z_in,
    load_sem, tok_recv, up_send, down_send, y_send, c_send, c_send_y,
    rc_send, rc_recv, ry_send, ry_recv, rz_send, rz_recv,
):
    me = lax.axis_index("expert")
    z, y, c = me // 4, (me // 2) % 2, me % 2
    half = z // 2
    near = z + half * (3 - 2 * z)
    experts, _, slots = picks.shape
    rows, width = 2 * tokens.shape[1], tokens.shape[2]
    expert = me // 2
    y_peer, c_peer = me + 2 - 4 * y, me + 1 - 2 * c

    def mirror(o):
        return o + half * (3 - 2 * o)

    arrive = [mirror(near), mirror(1 - near), mirror(2), mirror(3)]
    leave = [arrive[2], arrive[3], arrive[1], arrive[0]]

    own = pltpu.make_async_copy(tokens, tok.at[me, :, :, :width], load_sem.at[6])
    own.start()
    loads = [
        pltpu.make_async_copy(src, dst, load_sem.at[i])
        for i, (src, dst) in enumerate(
            [
                (shared_gate, w_gate),
                (shared_up, w_up),
                (slab_gate.at[0], r_gate),
                (slab_up.at[0], r_up),
                (slab_down.at[0], r_down),
                (shared_down, w_down),
            ]
        )
    ]
    barrier = pltpu.get_barrier_semaphore()

    def greet(target):
        pl.semaphore_signal(barrier, inc=1, device_id={"expert": target})

    greet(y_peer)
    greet(c_peer)

    @pl.when(z < LINE - 1)
    def _():
        greet(me + 4)

    @pl.when(z > 0)
    def _():
        greet(me - 4)

    meta = routing_columns(picks, counts, gates, rows)
    own.wait()
    tok[me, :, :, width:] = meta.reshape(2, rows // 2, LANES)
    pl.semaphore_wait(barrier, 3 + near)

    def block_copy(s, h, target, send_sem):
        return pltpu.make_async_remote_copy(
            src_ref=tok.at[s, h], dst_ref=tok.at[s, h], send_sem=send_sem, recv_sem=tok_recv.at[s, h],
            device_id={"expert": target},
        )

    def column_copies(zt, h, act):
        s = zt * 4 + y * 2 + c

        @pl.when((zt <= z) & (z < LINE - 1))
        def _():
            act(block_copy(s, h, me + 4, up_send.at[zt, h]))

        @pl.when((zt >= z) & (z > 0))
        def _():
            act(block_copy(s, h, me - 4, down_send.at[zt, h]))

        act(block_copy(s, h, y_peer, y_send.at[zt, h]))
        act(block_copy(s, h, c_peer, c_send.at[zt, h]))

    def start(copy):
        copy.start()

    def wait_send(copy):
        copy.wait_send()

    def got(s, h):
        block_copy(s, h, c_peer, c_send.at[0, 0]).wait_recv()

    def line_step(zt, h):
        got(zt * 4 + y * 2 + c, h)
        column_copies(zt, h, start)

    def y_step(zt, h):
        s = zt * 4 + (1 - y) * 2 + c
        got(s, h)
        block_copy(s, h, c_peer, c_send_y.at[zt, h]).start()

    def core_step(zt):
        for h in range(2):
            got(zt * 4 + 1 - c, h)
            got(zt * 4 + 3 - c, h)

    def first_half(i):
        zt = arrive[i]

        def tile(n, _):
            columns = pl.ds(pl.multiple_of(n * 256, 256), 256)
            x = tok[pl.ds(zt * 4, 4), :, :, :width].reshape(4 * rows, width)
            g = dot(x, w_gate[:, columns])
            u = dot(x, w_up[:, columns])
            hidden[zt, :, columns] = silu_mul(g, u).astype(BF16)
            return 0

        lax.fori_loop(0, w_gate.shape[1] // 256, tile, 0, unroll=True)
        info = tok[pl.ds(zt * 4, 4), :, :, width:].reshape(4 * rows, LANES)
        slots4 = 4 * slots
        lane_r = lax.broadcasted_iota(jnp.int32, (slots4, LANES), 1)
        pick_code = jnp.where(lane_r == experts + expert, 1.0, 0.0).astype(BF16)
        pick_weight = jnp.where(lane_r == expert, 1.0, 0.0).astype(BF16)
        nt = (((1,), (1,)), ((), ()))
        code_t = lax.dot_general(pick_code, info, nt, preferred_element_type=F32)
        code = lax.dot_general(info, pick_code, nt, preferred_element_type=F32)
        weight = lax.dot_general(info, pick_weight, nt, preferred_element_type=F32)

        def match(codes, slot_dim):
            slot = lax.broadcasted_iota(jnp.int32, codes.shape, slot_dim)
            token = lax.broadcasted_iota(jnp.int32, codes.shape, 1 - slot_dim)
            return (codes == (slot % slots + 1).astype(F32)) & (slot // slots == token // rows)

        scatter[zt] = jnp.where(match(code, 1), weight, 0.0).astype(BF16)
        gather = jnp.where(match(code_t, 0), 1.0, 0.0).astype(BF16)
        x = tok[pl.ds(zt * 4, 4), :, :, :width].reshape(4 * rows, width)
        routed_x[i * 4 * slots : (i + 1) * 4 * slots] = dot(gather, x).astype(BF16)

    picked = 4 * slots
    hs = r_gate.shape[1]

    def routed(first, count):
        size = count * picked
        base = first * picked
        for low in range(0, hs, 256):
            high = min(hs, low + 256)
            g = dot(routed_x[base : base + size], r_gate[:, low:high])
            u = dot(routed_x[base : base + size], r_up[:, low:high])
            routed_hidden[:size, low:high] = silu_mul(g, u).astype(BF16)

        def tile(n, _):
            columns = pl.ds(pl.multiple_of(n * 256, 256), 256)
            o = dot(routed_hidden[:size], r_down[:, columns]).astype(BF16)
            routed_out[base : base + size, columns] = o
            return 0

        lax.fori_loop(0, width // 256, tile, 0, unroll=True)

    middle = width // 512 * 256
    cuts = ((0, middle), (middle, width - middle))

    def cut(h):
        return pl.ds(*cuts[h])

    def core_copy(zt, h):
        return pltpu.make_async_remote_copy(
            src_ref=part.at[zt, 1 - c, :, :, cut(h)], dst_ref=core_in.at[zt, :, :, cut(h)],
            send_sem=rc_send.at[zt, h], recv_sem=rc_recv.at[zt, h], device_id={"expert": c_peer},
        )

    def y_copy(zt, h):
        return pltpu.make_async_remote_copy(
            src_ref=y_out.at[zt, :, cut(h)], dst_ref=y_in.at[zt, :, cut(h)],
            send_sem=ry_send.at[zt, h], recv_sem=ry_recv.at[zt, h], device_id={"expert": y_peer},
        )

    def z_copy(zt, h, way, target):
        return pltpu.make_async_remote_copy(
            src_ref=z_out.at[zt, :, cut(h)], dst_ref=z_in.at[way, zt, :, cut(h)],
            send_sem=rz_send.at[zt, h], recv_sem=rz_recv.at[way, zt, h], device_id={"expert": target},
        )

    def second_half(i, h):
        zt = arrive[i]

        def tile(n, _):
            columns = pl.ds(pl.multiple_of(n * 256, 256), 256)
            p = dot(hidden[zt], w_down[:, columns]) + dot(scatter[zt], routed_out[i * picked : (i + 1) * picked, columns])
            p = p.astype(BF16)
            for b in range(4):
                part[zt, b % 2, b // 2, :, columns] = p[b * rows : (b + 1) * rows]
            return 0

        low, size = cuts[h]
        lax.fori_loop(low // 256, (low + size) // 256, tile, 0, unroll=True)
        core_copy(zt, h).start()

    def y_stage(zt, h):
        core_copy(zt, h).wait_recv()
        away = part[zt, c, 1 - y, :, cut(h)].astype(F32) + core_in[zt, 1 - y, :, cut(h)].astype(F32)
        y_out[zt, :, cut(h)] = away.astype(BF16)
        y_copy(zt, h).start()
        y_keep[zt, :, cut(h)] = (
            part[zt, c, y, :, cut(h)].astype(F32) + core_in[zt, y, :, cut(h)].astype(F32)
        )

    def z_stage(zt, h, last):
        y_copy(zt, h).wait_recv()
        y_keep[zt, :, cut(h)] += y_in[zt, :, cut(h)].astype(F32)

        @pl.when((zt >= z) & (z > 0))
        def _():
            z_copy(zt, h, 0, me - 4).wait_recv()
            y_keep[zt, :, cut(h)] += z_in[0, zt, :, cut(h)].astype(F32)

        @pl.when((zt <= z) & (z < LINE - 1))
        def _():
            z_copy(zt, h, 1, me + 4).wait_recv()
            y_keep[zt, :, cut(h)] += z_in[1, zt, :, cut(h)].astype(F32)

        if last:
            out[:, cut(h)] = y_keep[zt, :, cut(h)].astype(BF16)
        else:
            z_out[zt, :, cut(h)] = y_keep[zt, :, cut(h)].astype(BF16)

            @pl.when(zt > z)
            def _():
                z_copy(zt, h, 0, me + 4).start()

            @pl.when(zt < z)
            def _():
                z_copy(zt, h, 1, me - 4).start()

    for h in range(2):
        column_copies(arrive[0], h, start)
    for load in loads:
        load.start()
    for h in range(2):
        line_step(arrive[1], h)

        @pl.when(near == 1)
        def _():
            line_step(arrive[2], h)

        y_step(arrive[0], h)
    core_step(arrive[0])
    loads[0].wait()
    loads[1].wait()
    first_half(0)

    for h in range(2):
        line_step(mirror(2 + near), h)
    for h in range(2):
        y_step(arrive[1], h)
    core_step(arrive[1])
    first_half(1)
    for load in loads[2:5]:
        load.wait()

    for h in range(2):

        @pl.when(near == 0)
        def _():
            line_step(arrive[3], h)

        y_step(arrive[2], h)
    core_step(arrive[2])
    first_half(2)
    for h in range(2):
        y_step(arrive[3], h)
    routed(0, 3)
    loads[5].wait()
    second_half(2, 0)
    second_half(2, 1)
    for h in range(2):
        y_stage(arrive[2], h)
    core_step(arrive[3])
    first_half(3)
    routed(3, 1)
    second_half(3, 0)
    second_half(3, 1)
    y_stage(arrive[3], 0)
    second_half(1, 0)
    y_stage(arrive[3], 1)
    second_half(1, 1)
    y_stage(arrive[1], 0)

    @pl.when(near == 0)
    def _():
        for h in range(2):
            z_stage(arrive[2], h, False)

    second_half(0, 0)
    y_stage(arrive[1], 1)
    second_half(0, 1)
    y_stage(arrive[0], 0)
    y_stage(arrive[0], 1)

    @pl.when(near == 1)
    def _():
        for h in range(2):
            z_stage(arrive[2], h, False)

    for i in range(1, LINE):
        for h in range(2):
            z_stage(leave[i], h, i == LINE - 1)

    for i in range(LINE):
        for h in range(2):
            column_copies(arrive[i], h, wait_send)
            s = arrive[i] * 4 + (1 - y) * 2 + c
            block_copy(s, h, c_peer, c_send_y.at[arrive[i], h]).wait_send()
            core_copy(leave[i], h).wait_send()
            y_copy(leave[i], h).wait_send()
            if i < LINE - 1:
                z_copy(leave[i], h, 0, y_peer).wait_send()


def fused(
    tokens, shared_gate, shared_up, shared_down, slab_gate, slab_up, slab_down, picks, counts, gates
):
    rows, width = tokens.shape
    hid = shared_gate.shape[1]
    hs = slab_gate.shape[2]
    slots = picks.shape[2]
    any_spec = pl.BlockSpec(memory_space=pl.ANY)
    vmem_spec = pl.BlockSpec(memory_space=pltpu.VMEM)
    dma = pltpu.SemaphoreType.DMA
    vm = pltpu.VMEM
    flops = 2 * 16 * rows * width * hid * 3
    return pl.pallas_call(
        kernel,
        out_shape=jax.ShapeDtypeStruct((rows, width), BF16),
        in_specs=[any_spec] * 7 + [vmem_spec] * 3,
        out_specs=vmem_spec,
        scratch_shapes=[
            vm((width, hid), BF16), vm((width, hid), BF16), vm((hid, width), BF16),
            vm((width, hs), BF16), vm((width, hs), BF16), vm((hs, width), BF16),
            vm((4 * LINE, 2, rows // 2, width + LANES), BF16),
            vm((LINE, 4 * rows, hid), BF16),
            vm((LINE * 4 * slots, width), BF16),
            vm((LINE * 4 * slots, hs), BF16),
            vm((LINE * 4 * slots, width), BF16),
            vm((LINE, 4 * rows, 4 * slots), BF16),
            vm((LINE, 2, 2, rows, width), BF16),
            vm((LINE, 2, rows, width), BF16),
            vm((LINE, rows, width), BF16),
            vm((LINE, rows, width), BF16),
            vm((LINE, rows, width), F32),
            vm((LINE, rows, width), BF16),
            vm((2, LINE, rows, width), BF16),
            dma((7,)), dma((4 * LINE, 2)), dma((LINE, 2)), dma((LINE, 2)), dma((LINE, 2)),
            dma((LINE, 2)), dma((LINE, 2)),
            dma((LINE, 2)), dma((LINE, 2)), dma((LINE, 2)), dma((LINE, 2)), dma((LINE, 2)),
            dma((2, LINE, 2)),
        ],
        compiler_params=pltpu.CompilerParams(
            collective_id=0, has_side_effects=True, vmem_limit_bytes=60 * 1024 * 1024
        ),
        cost_estimate=pl.CostEstimate(flops=flops, bytes_accessed=21000000, transcendentals=0),
    )(tokens.reshape(2, rows // 2, width), shared_gate, shared_up, shared_down, slab_gate, slab_up, slab_down, picks, counts, gates)


def return_routed(contribution, sources, slot_count, features, onehot, experts, tok_dev):
    returned = lax.all_to_all(
        contribution.reshape(sources, slot_count, features),
        "expert",
        split_axis=0,
        concat_axis=0,
        tiled=True,
    )
    owner_table = (
        jnp.repeat(onehot, 2, axis=0)
        .reshape(2 * experts * slot_count, tok_dev)
        .astype(jnp.bfloat16)
    )
    return lax.dot_general(
        owner_table,
        returned.reshape(-1, features),
        (((0,), (0,)), ((), ())),
        preferred_element_type=jnp.float32,
    )


def on_device(
    tokens, shared_gate, shared_up, shared_down, slab_gate, slab_up, slab_down, picks, counts, gates
):
    tok_dev, features = tokens.shape
    own_picks = picks[:, 0, :]
    own_gates = gates[:, 0, :]
    experts, slot_count = own_picks.shape
    live_slot = lax.broadcasted_iota(jnp.int32, (experts, slot_count), 1) < counts
    local_rows = lax.broadcasted_iota(jnp.int32, (1, 1, tok_dev), 2)
    onehot = (own_picks[:, :, None] == local_rows) & live_slot[:, :, None]
    gate_total = jnp.sum(jnp.where(onehot, own_gates[:, :, None], 0.0), axis=(0, 1))
    divisor = jnp.maximum(gate_total, 1.0)
    weight = jnp.where(live_slot, own_gates / divisor[own_picks], 0.0).astype(jnp.bfloat16)
    sent_rows = jnp.where(live_slot[:, :, None], tokens[own_picks], jnp.zeros((), tokens.dtype))
    positions = own_picks.astype(jnp.float32).astype(jnp.bfloat16)
    weight_both = jnp.repeat(weight, 2, axis=0)
    position_both = jnp.repeat(positions, 2, axis=0)
    received, got_weight, got_position = (
        lax.all_to_all(
            jnp.repeat(sent_rows, 2, axis=0), "expert", split_axis=0, concat_axis=0, tiled=True
        ),
        lax.all_to_all(weight_both, "expert", split_axis=0, concat_axis=0, tiled=True),
        lax.all_to_all(position_both, "expert", split_axis=0, concat_axis=0, tiled=True),
    )
    sources = received.shape[0]
    flat_rows = received.reshape(sources * slot_count, features)
    gate_act = jnp.dot(flat_rows, slab_gate[0], preferred_element_type=jnp.float32)
    up_act = jnp.dot(flat_rows, slab_up[0], preferred_element_type=jnp.float32)
    slab_hidden = (jax.nn.silu(gate_act) * up_act).astype(jnp.bfloat16)
    slab_output = jnp.dot(slab_hidden, slab_down[0], preferred_element_type=jnp.float32)
    contribution = (slab_output * got_weight.reshape(-1, 1).astype(jnp.float32)).astype(
        jnp.bfloat16
    )
    piece = lax.all_gather(tokens, "expert", axis=0, tiled=True)
    gate_part = jnp.dot(piece, shared_gate, preferred_element_type=jnp.float32)
    up_part = jnp.dot(piece, shared_up, preferred_element_type=jnp.float32)
    shared_hidden = (jax.nn.silu(gate_part) * up_part).astype(jnp.bfloat16)
    layer_sum = lax.psum_scatter(
        jnp.dot(shared_hidden, shared_down, preferred_element_type=jnp.float32),
        "expert",
        scatter_dimension=0,
        tiled=True,
    )
    layer_sum = layer_sum + return_routed(
        contribution, sources, slot_count, features, onehot, experts, tok_dev
    )
    return layer_sum.astype(jnp.bfloat16)


def solution(mesh):
    in_specs = (
        P(("group", "expert"), None),
        P(None, "expert"),
        P(None, "expert"),
        P("expert", None),
        P("expert", None, None),
        P("expert", None, None),
        P("expert", None, None),
        P("group", "expert", None),
        P("group", "expert"),
        P("group", "expert", None),
    )
    out_specs = P(("group", "expert"), None)
    body = fused if mesh.shape["expert"] == 4 * LINE else on_device
    return jax.shard_map(
        body, mesh=mesh, in_specs=in_specs, out_specs=out_specs, check_vma=False
    )
```
